32 devices in a mesh: row: 8 (over z, y), col: 4 (over x, core).
Axes of the slice: x: 2, y: 2, z: 4, core: 2. Of those that a mesh axis runs over, the one named last changes fastest.
Arguments:
- inputs: bfloat16 [512, 12288], P('row', 'col'), may hold values from -6 to 6
- hidden_pre: bfloat16 [512, 24576], P(None, 'row'), may hold values from -8 to 8
- out_grad: bfloat16 [512, 12288], P('row', 'col'), may hold values from -6 to 6
- weight_in: bfloat16 [12288, 24576], P('col', 'row'), may hold values from -0.0546875 to 0.0546875
- weight_out: bfloat16 [24576, 12288], P('row', 'col'), may hold values from -0.0390625 to 0.0390625
Outputs:
- grad_in: bfloat16 [512, 12288], P('row', 'col')
- grad_weight_in: bfloat16 [12288, 24576], P('col', 'row')
- grad_weight_out: bfloat16 [24576, 12288], P('row', 'col')
The draws below stay inside these ranges and needn't reach their ends.
All inputs are finite; a program needn't handle non-finite values.
Results may differ from the reference program's by a relative error of at most 0.0049.
Values may be sent and summed in bfloat16 or wider, within the bound.
No kernel may reach another device: no remote copies, remote signals or barrier semaphores. Data moves between devices by JAX's collectives and lax.ppermute only.
A program may use at most 192 MiB of HBM per device.

```python
import jax
import jax.numpy as jnp

D = 12288
FF = 24576
TOKENS = 512


def level_of(rng, shape, shards, low, top_value):
    gain, own = 1.0, jax.random.fold_in(rng, 6)
    for dim, blocks in shards:
        draws = jnp.exp(jax.random.uniform(jax.random.fold_in(own, dim), (blocks,), jnp.float32, low / len(shards), top_value / len(shards)))
        gain = gain * jnp.repeat(draws, shape[dim] // blocks).reshape([-1 if axis == dim else 1 for axis in range(len(shape))])
    return gain


def normal_values(stream_key, dims, width, reach, pieces=(), kind=jnp.bfloat16):
    drawn = jax.random.normal(stream_key, dims, jnp.float32) * width
    if len(pieces) > 0:
        drawn = level_of(stream_key, dims, pieces, -0.22, 0.18) * drawn
    return jnp.clip(drawn, min=-reach, max=reach).astype(kind)


def setup_inputs(seed: int = 0) -> dict:
    seeds = jax.random.split(jax.random.key(seed), 6)
    inputs = normal_values(seeds[0], (TOKENS, D), 1.0, 6.0, ((0, 8), (1, 4)))
    hidden_pre = normal_values(seeds[1], (TOKENS, FF), 1.5, 8.0, ((1, 8),))
    out_grad = normal_values(seeds[2], (TOKENS, D), 1.0, 6.0, ((0, 8), (1, 4)))
    weight_in = normal_values(seeds[3], (D, FF), D ** -0.5, 0.0546875, ((0, 4), (1, 8)))
    weight_out = normal_values(seeds[4], (FF, D), FF ** -0.5, 0.0390625, ((0, 8), (1, 4)))
    return {"inputs": inputs, "hidden_pre": hidden_pre, "out_grad": out_grad, "weight_in": weight_in, "weight_out": weight_out}


def gelu_parts(hidden_pre):
    hval = hidden_pre.astype(jnp.float32)
    inner = 0.7978845608 * (hval + 0.044715 * hval * hval * hval)
    tval = jnp.tanh(inner)
    act = 0.5 * hval * (1.0 + tval)
    slope = 0.5 * (1.0 + tval) + 0.5 * hval * (1.0 - tval * tval) * 0.7978845608 * (1.0 + 3.0 * 0.044715 * hval * hval)
    return act, slope


def reference(inputs, hidden_pre, out_grad, weight_in, weight_out):
    act, slope = gelu_parts(hidden_pre)
    act_b = act.astype(jnp.bfloat16)
    d_act = jnp.dot(out_grad, weight_out.T, preferred_element_type=jnp.float32)
    d_hid = (d_act * slope).astype(jnp.bfloat16)
    grad_weight_out = jnp.dot(act_b.T, out_grad, preferred_element_type=jnp.float32).astype(jnp.bfloat16)
    grad_in = jnp.dot(d_hid, weight_in.T, preferred_element_type=jnp.float32).astype(jnp.bfloat16)
    grad_weight_in = jnp.dot(inputs.T, d_hid, preferred_element_type=jnp.float32).astype(jnp.bfloat16)
    return grad_in, grad_weight_in, grad_weight_out
```

```python
import functools

import jax
import jax.numpy as jnp
from jax import lax
from jax.experimental import pallas as pl
from jax.experimental.pallas import tpu as pltpu
from jax.sharding import PartitionSpec as P

VMEM_BYTES = 48 * 2**20


def row_cycle(mesh):
    first = mesh.devices[:, 0]
    places = [getattr(device, "coords", None) for device in first]
    if any(place is None for place in places):
        return list(range(len(first)))
    at = {(place[2], place[1]): index for index, place in enumerate(places)}
    zs, ys = (sorted({key[i] for key in at}) for i in (0, 1))
    if len(at) != len(places) or len(at) != len(zs) * len(ys) or len(ys) < 2:
        return list(range(len(first)))
    walk = []
    for step, z in enumerate(zs):
        walk += [at[z, y] for y in (ys[1:] if step % 2 == 0 else ys[:0:-1])]
    return walk + [at[z, ys[0]] for z in reversed(zs)]


def pieces_of(length, want):
    return max(n for n in range(1, want + 1) if length % (128 * n) == 0 or n == 1)


def tile_of(length, most):
    return max(t for t in range(1, most + 1) if length % t == 0 and (t % 128 == 0 or t == length))


def gelu_parts(hidden_pre):
    hval = hidden_pre.astype(jnp.float32)
    inner = 0.7978845608 * (hval + 0.044715 * hval * hval * hval)
    tval = jnp.tanh(inner)
    act = 0.5 * hval * (1.0 + tval)
    slope = 0.5 * (1.0 + tval) + 0.5 * hval * (1.0 - tval * tval) * 0.7978845608 * (
        1.0 + 3.0 * 0.044715 * hval * hval
    )
    return (act, slope)


def gelu_piece(order, hidden_pre, count, part, parts, held):
    tokens, hidden = hidden_pre.shape
    share = tokens // count
    half = hidden // 2
    steps = count // parts
    first = part * steps

    def kernel(order_ref, h_ref, *refs):
        act_ref, slope_ref = refs[-2:]
        for index in range(2):
            act, slope = gelu_parts(h_ref[:, index * half : (index + 1) * half])
            act_ref[:, index * half : (index + 1) * half] = act.astype(jnp.bfloat16)

            @pl.when(order_ref[count] == index)
            def _():
                slope_ref[...] = slope

    return pl.pallas_call(
        kernel,
        grid_spec=pltpu.PrefetchScalarGridSpec(
            num_scalar_prefetch=1,
            grid=(steps,),
            in_specs=[pl.BlockSpec((share, hidden), lambda i, s: (s[first + i], 0))]
            + ([] if held is None else [pl.BlockSpec(memory_space=pl.ANY)] * 2),
            out_specs=[
                pl.BlockSpec((share, hidden), lambda i, s: (first + i, 0)),
                pl.BlockSpec((share, half), lambda i, s: (first + i, 0)),
            ],
        ),
        out_shape=[
            jax.ShapeDtypeStruct((tokens, hidden), jnp.bfloat16),
            jax.ShapeDtypeStruct((tokens, half), jnp.float32),
        ],
        input_output_aliases={} if held is None else {2: 0, 3: 1},
        compiler_params=pltpu.CompilerParams(vmem_limit_bytes=VMEM_BYTES),
        cost_estimate=cost(20 * tokens * hidden // parts, 6 * tokens * hidden // parts),
        name="gelu_piece",
    )(order, hidden_pre, *(held or ()))


def after(value, *others):
    return lax.optimization_barrier((value, *others))[0]


def ring_gather(value, cycle):
    count = len(cycle)
    ahead = [(cycle[i], cycle[(i + 1) % count]) for i in range(count)]
    behind = [(b, a) for a, b in ahead]
    blocks = {0: value}
    state = [value, value]

    def step(k, *others):
        fore, back = state
        if 2 * k == count:
            cut = value.shape[0] // 2
            fore, back = fore[:cut], back[cut:]
        if others:
            fore, back = lax.optimization_barrier((fore, back, *others))[:2]
        state[:] = lax.ppermute(fore, "row", ahead), lax.ppermute(back, "row", behind)
        if 2 * k == count:
            blocks[k] = jnp.concatenate(state, 0)
        else:
            blocks[count - k], blocks[k] = state

    return step, lambda: jnp.concatenate([blocks[k] for k in range(count)], 0)


def ring_sum(partial, cycle, dtype, fill):
    count = len(cycle)
    share = partial.shape[0] // count
    width = partial.shape[1]
    half = width // 2
    ahead = [(cycle[i], cycle[(i + 1) % count]) for i in range(count)]
    behind = [(b, a) for a, b in ahead]

    def block(shift):
        start = shift % count * share
        return partial[start : start + share]

    def plus(left, right):
        return left.astype(jnp.float32) + right.astype(jnp.float32)

    def move(first, second):
        sent = (first.astype(jnp.bfloat16), second.astype(jnp.bfloat16))
        return fill(sent, (lax.ppermute(sent[0], "row", ahead), lax.ppermute(sent[1], "row", behind)))

    most = count // 2
    if count == 1:
        return partial.astype(dtype)
    fore = back = None
    if count % 2 == 0:
        far = block(most)
        fore, back = move(far[:, :half], far[:, half:])
        most -= 1
    for shift in range(most, 0, -1):
        first, second = block(shift), block(-shift)
        if fore is not None and fore.shape[1] < width:
            first = jnp.concatenate([plus(first[:, :half], fore), first[:, half:]], 1)
            second = jnp.concatenate([second[:, :half], plus(second[:, half:], back)], 1)
        elif fore is not None:
            first, second = plus(first, fore), plus(second, back)
        fore, back = move(first, second)
    own = block(0)
    if fore.shape[1] < width:
        return jnp.concatenate([plus(own[:, :half], fore), plus(own[:, half:], back)], 1).astype(dtype)
    return (plus(own, fore) + back.astype(jnp.float32)).astype(dtype)


def cost(flops, moved):
    return pl.CostEstimate(flops=flops, bytes_accessed=moved, transcendentals=0)


def act_grad_piece(start, grads, weight_out, width, dtype):
    tokens, depth = grads.shape
    tile = tile_of(width, 256)

    def kernel(_, g_ref, w_ref, o_ref):
        o_ref[...] = lax.dot_general(
            g_ref[...], w_ref[...], (((1,), (1,)), ((), ())), preferred_element_type=jnp.float32
        ).astype(dtype)

    return pl.pallas_call(
        kernel,
        grid_spec=pltpu.PrefetchScalarGridSpec(
            num_scalar_prefetch=1,
            grid=(width // tile,),
            in_specs=[
                pl.BlockSpec((tokens, depth), lambda i, s: (0, 0)),
                pl.BlockSpec((tile, depth), lambda i, s: (s[0] * (width // tile) + i, 0)),
            ],
            out_specs=pl.BlockSpec((tokens, tile), lambda i, s: (0, i)),
        ),
        out_shape=jax.ShapeDtypeStruct((tokens, width), dtype),
        compiler_params=pltpu.CompilerParams(vmem_limit_bytes=VMEM_BYTES),
        cost_estimate=cost(2 * tokens * depth * width, 2 * width * depth + 4 * tokens * width),
        name="act_grad_piece",
    )(start, grads, weight_out)


def input_grad_piece(where, mine, other, weight_in, total, dtype):
    tokens, width = mine.shape
    out = weight_in.shape[0]
    tile = tile_of(out, 512)

    def kernel(_, m_ref, o_ref, wm_ref, wo_ref, *refs):
        dims = (((1,), (1,)), ((), ()))
        value = lax.dot_general(m_ref[...], wm_ref[...], dims, preferred_element_type=jnp.float32)
        value += lax.dot_general(o_ref[...], wo_ref[...], dims, preferred_element_type=jnp.float32)
        if len(refs) > 1:
            value += refs[0][...]
        refs[-1][...] = value.astype(dtype)

    block = pl.BlockSpec((tokens, tile), lambda i, s: (0, i))
    held = pl.BlockSpec((tokens, width), lambda i, s: (0, 0))
    return pl.pallas_call(
        kernel,
        grid_spec=pltpu.PrefetchScalarGridSpec(
            num_scalar_prefetch=1,
            grid=(out // tile,),
            in_specs=[
                held,
                held,
                pl.BlockSpec((tile, width), lambda i, s: (i, s[0])),
                pl.BlockSpec((tile, width), lambda i, s: (i, s[1])),
            ]
            + ([] if total is None else [block]),
            out_specs=block,
        ),
        out_shape=jax.ShapeDtypeStruct((tokens, out), dtype),
        compiler_params=pltpu.CompilerParams(vmem_limit_bytes=VMEM_BYTES),
        cost_estimate=cost(4 * tokens * width * out, 4 * width * out + 8 * tokens * out),
        name="input_grad_piece",
    )(where, mine, other, weight_in, weight_in, *([] if total is None else [total]))


def weight_out_grad_piece(act, grads, part, parts, held):
    tokens, rows = act.shape
    columns = grads.shape[1]
    share = rows // parts
    tile = tile_of(share, 512)
    first = part * (share // tile)

    def kernel(a_ref, g_ref, *refs):
        refs[-1][...] = lax.dot_general(
            a_ref[...], g_ref[...], (((0,), (0,)), ((), ())), preferred_element_type=jnp.float32
        ).astype(jnp.bfloat16)

    return pl.pallas_call(
        kernel,
        grid=(share // tile,),
        in_specs=[
            pl.BlockSpec((tokens, tile), lambda i: (0, first + i)),
            pl.BlockSpec((tokens, columns), lambda i: (0, 0)),
        ]
        + ([] if held is None else [pl.BlockSpec(memory_space=pl.ANY)]),
        out_specs=pl.BlockSpec((tile, columns), lambda i: (first + i, 0)),
        out_shape=jax.ShapeDtypeStruct((rows, columns), jnp.bfloat16),
        input_output_aliases={} if held is None else {2: 0},
        compiler_params=pltpu.CompilerParams(vmem_limit_bytes=VMEM_BYTES),
        cost_estimate=cost(2 * tokens * share * columns, 2 * share * columns + 2 * tokens * columns),
        name="weight_out_grad_piece",
    )(act, grads, *([] if held is None else [held]))


def weight_in_grad_piece(where, inputs, hid_pieces, part, parts, held):
    tokens, rows = inputs.shape
    count = len(hid_pieces)
    width = hid_pieces[0].shape[1]
    columns = width * count
    share = rows // parts
    tile = tile_of(share, 512)
    first = part * (share // tile)

    def kernel(where_ref, i_ref, *refs):
        left = i_ref[...].T
        for index in range(count):
            at = pl.multiple_of(where_ref[index] * width, 128)
            refs[-1][:, pl.ds(at, width)] = jnp.dot(
                left, refs[index][...], preferred_element_type=jnp.float32
            ).astype(jnp.bfloat16)

    return pl.pallas_call(
        kernel,
        grid_spec=pltpu.PrefetchScalarGridSpec(
            num_scalar_prefetch=1,
            grid=(share // tile,),
            in_specs=[pl.BlockSpec((tokens, tile), lambda i, s: (0, first + i))]
            + [pl.BlockSpec((tokens, width), lambda i, s: (0, 0))] * count
            + ([] if held is None else [pl.BlockSpec(memory_space=pl.ANY)]),
            out_specs=pl.BlockSpec((tile, columns), lambda i, s: (first + i, 0)),
        ),
        out_shape=jax.ShapeDtypeStruct((rows, columns), jnp.bfloat16),
        input_output_aliases={} if held is None else {2 + count: 0},
        compiler_params=pltpu.CompilerParams(vmem_limit_bytes=VMEM_BYTES),
        cost_estimate=cost(2 * tokens * share * columns, 2 * share * columns + 4 * tokens * columns),
        name="weight_in_grad_piece",
    )(where, inputs, *hid_pieces, *([] if held is None else [held]))


def body(cycle, inputs, hidden_pre, out_grad, weight_in, weight_out):
    cols = lax.axis_size("col")
    core = lax.axis_index("col") % 2
    twin = [(i, i ^ 1) for i in range(cols)]
    hops = [[(i, (i + 2 * hop) % cols) for i in range(cols)] for hop in range(1, cols // 2)]
    rows = len(cycle)
    place = lax.axis_index("row")
    order = [
        sum(jnp.where(place == row, cycle[(spot + shift) % rows], 0) for spot, row in enumerate(cycle))
        for shift in range(rows)
    ]
    half = hidden_pre.shape[1] // 2
    parts = pieces_of(half, 2)
    width = half // parts

    def at(*indices):
        return jnp.stack(indices).astype(jnp.int32)

    cut = out_grad.shape[1] // 2
    lanes = [ring_gather(out_grad[:, :cut], cycle), ring_gather(out_grad[:, cut:], cycle)]
    order = at(*order, core)
    gelu, runs = None, max(n for n in (1, 2) if rows % n == 0)
    for k in range(1, rows // 2 + 1):
        for step, _ in lanes:
            step(k)
        if k <= runs:
            gelu = gelu_piece(order, hidden_pre, rows, k - 1, runs, gelu)
    grad_all = jnp.concatenate([whole() for _, whole in lanes], 1)
    act, slope = gelu
    grad_all, act, slope = lax.optimization_barrier((grad_all, act, slope))
    input_step, input_whole = ring_gather(inputs, cycle)
    due = list(range(1, rows // 2 + 1))

    def input_steps(count, *others):
        for _ in range(min(count, len(due))):
            input_step(due.pop(0), *others)

    sums, arrived, last = [], [], grad_all
    for part in range(parts):
        start = after(at((1 - core) * parts + part), last)
        given = act_grad_piece(start, grad_all, weight_out, width, jnp.bfloat16)
        taken = lax.ppermute(given, "col", twin)
        start = after(at(core * parts + part), given)
        kept = act_grad_piece(start, grad_all, weight_out, width, jnp.float32)
        total = kept + taken.astype(jnp.float32)
        last = total.astype(jnp.bfloat16)
        if part == 0:
            input_steps(rows // 8, given)
        sums.append(total)
        arrived.append([lax.ppermute(last, "col", hop) for hop in hops])

    input_steps(rows // 8, last)
    grad_weight_out = weight_out_grad_piece(after(act, last), grad_all, 0, 2, None)

    hid_pieces, where, partial = [], [], None
    for part in range(parts):
        if part == 0:
            arrived[part], grad_weight_out = lax.optimization_barrier((arrived[part], grad_weight_out))
        else:
            arrived[part], partial = lax.optimization_barrier((arrived[part], partial))
        total = sums[part]
        for value in arrived[part]:
            total = total + value.astype(jnp.float32)
        mine = (total * slope[:, part * width : (part + 1) * width]).astype(jnp.bfloat16)
        other = lax.ppermute(mine, "col", twin)
        here = [core * parts + part, (1 - core) * parts + part]
        place_here = at(*here)
        if part == 0:
            input_steps(rows // 8, mine)
            grad_weight_out = weight_out_grad_piece(after(act, mine), grad_all, 1, 2, grad_weight_out)
            place_here, grad_weight_out = lax.optimization_barrier((place_here, grad_weight_out))
        if part == 0:
            input_steps(rows, place_here)
        partial = input_grad_piece(place_here, mine, other, weight_in, partial, jnp.float32)
        hid_pieces += [mine, other]
        where += here

    input_all = input_whole()

    tiles = inputs.shape[1] // tile_of(inputs.shape[1], 512)
    slots = max(n for n in range(1, 4) if tiles % n == 0)
    state = {"next": 0, "grad": None}

    def fill(sent, received):
        if state["next"] == slots:
            return received
        state["grad"] = weight_in_grad_piece(
            after(at(*where), *sent), input_all, hid_pieces, state["next"], slots, state["grad"]
        )
        state["next"] += 1
        received, state["grad"] = lax.optimization_barrier((received, state["grad"]))
        return received

    grad_in = ring_sum(partial, cycle, jnp.bfloat16, fill)
    while state["next"] < slots:
        fill([], [])
    return (grad_in, state["grad"], grad_weight_out)


def solution(mesh):
    return jax.shard_map(
        functools.partial(body, row_cycle(mesh)),
        mesh=mesh,
        in_specs=(
            P("row", "col"),
            P(None, "row"),
            P("row", "col"),
            P("col", "row"),
            P("row", "col"),
        ),
        out_specs=(P("row", "col"), P("col", "row"), P("row", "col")),
        check_vma=False,
    )
```

```python
import functools

import jax
import jax.numpy as jnp
from jax import lax
from jax.experimental import pallas as pl
from jax.experimental.pallas import tpu as pltpu
from jax.sharding import PartitionSpec as P

VMEM_BYTES = 20 * 2**20
STREAM_VMEM_BYTES = 47 * 2**20


def row_cycle(mesh):
    first = mesh.devices[:, 0]
    places = [getattr(device, "coords", None) for device in first]
    if any(place is None for place in places):
        return list(range(len(first)))
    at = {(place[2], place[1]): index for index, place in enumerate(places)}
    zs, ys = (sorted({key[i] for key in at}) for i in (0, 1))
    if len(at) != len(places) or len(at) != len(zs) * len(ys) or len(ys) < 2:
        return list(range(len(first)))
    walk = []
    for step, z in enumerate(zs):
        walk += [at[z, y] for y in (ys[1:] if step % 2 == 0 else ys[:0:-1])]
    return walk + [at[z, ys[0]] for z in reversed(zs)]


def pieces_of(length, want):
    return max(n for n in range(1, want + 1) if length % (128 * n) == 0 or n == 1)


def tile_of(length, most):
    return max(t for t in range(1, most + 1) if length % t == 0 and (t % 128 == 0 or t == length))


def gelu_parts(hidden_pre):
    hval = hidden_pre.astype(jnp.float32)
    inner = 0.7978845608 * (hval + 0.044715 * hval * hval * hval)
    tval = jnp.tanh(inner)
    act = 0.5 * hval * (1.0 + tval)
    slope = 0.5 * (1.0 + tval) + 0.5 * hval * (1.0 - tval * tval) * 0.7978845608 * (
        1.0 + 3.0 * 0.044715 * hval * hval
    )
    return (act, slope)


def gelu_blocks(order, hidden_pre, count):
    tokens, hidden = hidden_pre.shape
    share = tokens // count
    half = hidden // 2

    def kernel(order_ref, h_ref, act_ref, slope_ref):
        for index in range(2):
            at = slice(index * half, (index + 1) * half)

            @pl.when(order_ref[count] == index)
            def _():
                act, slope = gelu_parts(h_ref[:, at])
                act_ref[:, at] = act.astype(jnp.bfloat16)
                slope_ref[...] = slope

            @pl.when(order_ref[count] != index)
            def _():
                act_ref[:, at] = gelu_parts(h_ref[:, at])[0].astype(jnp.bfloat16)

    return pl.pallas_call(
        kernel,
        grid_spec=pltpu.PrefetchScalarGridSpec(
            num_scalar_prefetch=1,
            grid=(count,),
            in_specs=[pl.BlockSpec((share, hidden), lambda i, s: (s[i], 0))],
            out_specs=[
                pl.BlockSpec((share, hidden), lambda i, s: (i, 0)),
                pl.BlockSpec((share, half), lambda i, s: (i, 0)),
            ],
        ),
        out_shape=[
            jax.ShapeDtypeStruct((tokens, hidden), jnp.bfloat16),
            jax.ShapeDtypeStruct((tokens, half), jnp.float32),
        ],
        compiler_params=pltpu.CompilerParams(vmem_limit_bytes=VMEM_BYTES),
        cost_estimate=cost(20 * tokens * hidden, 6 * tokens * hidden),
        name="gelu_blocks",
    )(order, hidden_pre)


def after(value, *others):
    return lax.optimization_barrier((value, *others))[0]


def ring_gather(value, cycle):
    count = len(cycle)
    ahead = [(cycle[i], cycle[(i + 1) % count]) for i in range(count)]
    behind = [(b, a) for a, b in ahead]
    blocks = {0: [value]}
    state = [value, value]

    def step(k, *others):
        fore, back = state
        if 2 * k == count:
            cut = value.shape[0] // 2
            fore, back = fore[:cut], back[cut:]
        if others:
            fore, back = lax.optimization_barrier((fore, back, *others))[:2]
        state[:] = lax.ppermute(fore, "row", ahead), lax.ppermute(back, "row", behind)
        share = value.shape[0]
        if 2 * k == count:
            blocks[k] = list(state)
            return [(k * share, state[0]), (k * share + cut, state[1])]
        blocks[count - k], blocks[k] = [state[0]], [state[1]]
        return [((count - k) * share, state[0]), (k * share, state[1])]

    return step, lambda: [piece for k in sorted(blocks) for piece in blocks[k]]


def ring_sum(block, cycle, share, width, dtype, fill):
    count = len(cycle)
    half = width // 2
    ahead = [(cycle[i], cycle[(i + 1) % count]) for i in range(count)]
    behind = [(b, a) for a, b in ahead]

    def plus(left, right):
        return left.astype(jnp.float32) + right.astype(jnp.float32)

    def move(first, second):
        sent = (first.astype(jnp.bfloat16), second.astype(jnp.bfloat16))
        return fill(sent, (lax.ppermute(sent[0], "row", ahead), lax.ppermute(sent[1], "row", behind)))

    most = count // 2
    if count == 1:
        return block(0).astype(dtype)
    fore = back = None
    if count % 2 == 0:
        far = block(most)
        fore, back = move(far[:, :half], far[:, half:])
        most -= 1
    for shift in range(most, 0, -1):
        first, second = block(shift), block(-shift)
        if fore is not None and fore.shape[1] < width:
            fore = jnp.pad(fore, ((0, 0), (0, width - half)))
            back = jnp.pad(back, ((0, 0), (half, 0)))
        if fore is not None:
            first, second = plus(first, fore), plus(second, back)
        fore, back = move(first, second)
    own = block(0)
    if fore.shape[1] < width:
        return jnp.concatenate([plus(own[:, :half], fore), plus(own[:, half:], back)], 1).astype(dtype)
    return (plus(own, fore) + back.astype(jnp.float32)).astype(dtype)


def cost(flops, moved):
    return pl.CostEstimate(flops=flops // 4, bytes_accessed=moved // 4, transcendentals=0)


NEAR = pl.BlockSpec(memory_space=pltpu.VMEM)
FAR = pl.BlockSpec(memory_space=pltpu.HBM)
SCALAR = pl.BlockSpec(memory_space=pltpu.SMEM)
LAST_DIMS = (((1,), (1,)), ((), ()))


def run_of(length, first):
    return [(0, first), (first, length - first)] if first < length else [(0, length)]


def act_grad_piece(start, grads, weight_out, width, dtype):
    tokens, depth = grads.shape
    runs = run_of(width, tile_of(width, 256))

    def kernel(start_ref, g_ref, w_ref, o_ref, near, sem):
        copies = [
            pltpu.make_async_copy(
                w_ref.at[pl.ds(pl.multiple_of(start_ref[0] * width + at, 128), size)],
                near.at[pl.ds(at, size)],
                sem.at[index],
            )
            for index, (at, size) in enumerate(runs)
        ]
        for copy in copies:
            copy.start()
        for copy, (at, size) in zip(copies, runs):
            copy.wait()
            o_ref[:, at : at + size] = lax.dot_general(
                g_ref[...], near[at : at + size, :], LAST_DIMS, preferred_element_type=jnp.float32
            ).astype(dtype)

    return pl.pallas_call(
        kernel,
        in_specs=[SCALAR, NEAR, FAR],
        out_specs=NEAR,
        out_shape=jax.ShapeDtypeStruct((tokens, width), dtype),
        scratch_shapes=[pltpu.VMEM((width, depth), jnp.bfloat16), pltpu.SemaphoreType.DMA((len(runs),))],
        compiler_params=pltpu.CompilerParams(vmem_limit_bytes=STREAM_VMEM_BYTES),
        cost_estimate=cost(2 * tokens * depth * width, 2 * width * depth + 4 * tokens * width),
        name="act_grad_piece",
    )(start, grads, weight_out)


def input_grad_piece(where, mine, other, weight_in, total, share, far):
    tokens, width = mine.shape
    out = weight_in.shape[0]
    tile = tile_of(out, 768)

    def kernel(_, m_ref, *refs):
        theirs = jnp.concatenate([ref[...] for ref in refs[: len(other)]], 0)
        wm_ref, wo_ref, *refs = refs[len(other) :]
        value = lax.dot_general(m_ref[...], wm_ref[...], LAST_DIMS, preferred_element_type=jnp.float32)
        value += lax.dot_general(theirs, wo_ref[...], LAST_DIMS, preferred_element_type=jnp.float32)
        if total is not None:
            value += refs[0][...]
            refs = refs[1:]
        refs[0][...] = value
        if far is not None:
            refs[1][...] = value[far * share : (far + 1) * share].astype(jnp.bfloat16)

    block = pl.BlockSpec((tokens, tile), lambda i, s: (0, i))
    out_specs, out_shape = [block], [jax.ShapeDtypeStruct((tokens, out), jnp.float32)]
    if far is not None:
        out_specs.append(pl.BlockSpec((share, tile), lambda i, s: (0, i)))
        out_shape.append(jax.ShapeDtypeStruct((share, out), jnp.bfloat16))
    return pl.pallas_call(
        kernel,
        grid_spec=pltpu.PrefetchScalarGridSpec(
            num_scalar_prefetch=1,
            grid=(out // tile,),
            in_specs=[NEAR] * (1 + len(other))
            + [
                pl.BlockSpec((tile, width), lambda i, s: (i, s[0])),
                pl.BlockSpec((tile, width), lambda i, s: (i, s[1])),
            ]
            + ([] if total is None else [block]),
            out_specs=out_specs,
        ),
        out_shape=out_shape,
        compiler_params=pltpu.CompilerParams(vmem_limit_bytes=STREAM_VMEM_BYTES),
        cost_estimate=cost(4 * tokens * width * out, 4 * width * out + 8 * tokens * out),
        name="input_grad_piece",
    )(where, mine, *other, weight_in, weight_in, *([] if total is None else [total]))


def weight_out_grad_piece(act, grads, part, parts, held):
    tokens, rows = act.shape
    columns = grads.shape[1]
    share = rows // parts
    tile = tile_of(share, 512)
    first = part * (share // tile)

    def kernel(a_ref, g_ref, *refs):
        refs[-1][...] = lax.dot_general(
            a_ref[...], g_ref[...], (((0,), (0,)), ((), ())), preferred_element_type=jnp.float32
        ).astype(jnp.bfloat16)

    return pl.pallas_call(
        kernel,
        grid=(share // tile,),
        in_specs=[
            pl.BlockSpec((tokens, tile), lambda i: (0, first + i)),
            NEAR,
        ]
        + ([] if held is None else [pl.BlockSpec(memory_space=pl.ANY)]),
        out_specs=pl.BlockSpec((tile, columns), lambda i: (first + i, 0)),
        out_shape=jax.ShapeDtypeStruct((rows, columns), jnp.bfloat16),
        input_output_aliases={} if held is None else {2: 0},
        compiler_params=pltpu.CompilerParams(vmem_limit_bytes=VMEM_BYTES),
        cost_estimate=cost(2 * tokens * share * columns, 2 * share * columns + 2 * tokens * columns),
        name="weight_out_grad_piece",
    )(act, grads, *([] if held is None else [held]))


def weight_in_grad_piece(where, input_pieces, hid_pieces, first, tiles, tile, held):
    rows = input_pieces[0].shape[1]
    tokens, width = hid_pieces[0][0].shape
    count, blocks = len(hid_pieces), len(input_pieces)
    hid_blocks = [block for piece in hid_pieces for block in piece]
    columns = width * count

    def kernel(where_ref, *refs):
        left = jnp.concatenate([ref[...] for ref in refs[:blocks]], 0).T
        spot = blocks
        for index, piece in enumerate(hid_pieces):
            at = pl.multiple_of(where_ref[index] * width, 128)
            right = jnp.concatenate([ref[...] for ref in refs[spot : spot + len(piece)]], 0)
            spot += len(piece)
            refs[-1][:, pl.ds(at, width)] = jnp.dot(left, right, preferred_element_type=jnp.float32).astype(
                jnp.bfloat16
            )

    return pl.pallas_call(
        kernel,
        grid_spec=pltpu.PrefetchScalarGridSpec(
            num_scalar_prefetch=1,
            grid=(tiles,),
            in_specs=[pl.BlockSpec((piece.shape[0], tile), lambda i, s: (0, first + i)) for piece in input_pieces]
            + [NEAR] * len(hid_blocks)
            + ([] if held is None else [pl.BlockSpec(memory_space=pl.ANY)]),
            out_specs=pl.BlockSpec((tile, columns), lambda i, s: (first + i, 0)),
        ),
        out_shape=jax.ShapeDtypeStruct((rows, columns), jnp.bfloat16),
        input_output_aliases={} if held is None else {1 + blocks + len(hid_blocks): 0},
        compiler_params=pltpu.CompilerParams(vmem_limit_bytes=VMEM_BYTES),
        cost_estimate=cost(2 * tokens * tiles * tile * columns, 2 * tiles * tile * columns),
        name="weight_in_grad_piece",
    )(where, *input_pieces, *hid_blocks, *([] if held is None else [held]))


def body(cycle, inputs, hidden_pre, out_grad, weight_in, weight_out):
    cols = lax.axis_size("col")
    core = lax.axis_index("col") % 2
    twin = [(i, i ^ 1) for i in range(cols)]
    hops = [[(i, (i + 2 * hop) % cols) for i in range(cols)] for hop in range(1, cols // 2)]
    rows, share = len(cycle), out_grad.shape[0]
    place = lax.axis_index("row")
    order = [
        sum(jnp.where(place == row, cycle[(spot + shift) % rows], 0) for spot, row in enumerate(cycle))
        for shift in range(rows)
    ]
    half = hidden_pre.shape[1] // 2
    parts = pieces_of(half, 2)
    width = half // parts

    def at(*indices):
        return jnp.stack(indices).astype(jnp.int32)

    steps = rows // 2
    order = at(*order, core)
    grad_step, grad_pieces = ring_gather(out_grad, cycle)
    grad_all = jnp.zeros((rows * share, out_grad.shape[1]), out_grad.dtype)

    def put(pieces):
        whole = grad_all
        for start, piece in pieces:
            whole = lax.dynamic_update_slice_in_dim(whole, piece, start, 0)
        return whole

    new = [(0, out_grad)]
    act = slope = None
    for k in range(1, steps + 1):
        fresh = grad_step(k, *([] if k == 1 else [act, slope, grad_all]))
        if k == 1:
            act, slope = gelu_blocks(order, hidden_pre, rows)
        grad_all = put(new)
        new = fresh
    grad_all = put(new)
    grad_all, act, slope = lax.optimization_barrier((grad_all, act, slope))
    input_step, input_pieces = ring_gather(inputs, cycle)
    due = list(range(1, steps + 1))

    quarter = max(1, steps // 4)

    def input_steps(count, *others):
        for _ in range(min(count, len(due))):
            input_step(due.pop(0), *others)

    given, last = [], grad_all
    for part in range(parts):
        last = act_grad_piece(after(at((1 - core) * parts + part), last), grad_all, weight_out, width, jnp.bfloat16)
        given.append(lax.ppermute(last, "col", twin))
    input_steps(quarter, last)
    sums, arrived = [], []
    for part in range(parts):
        start = after(at(core * parts + part), last)
        total = act_grad_piece(start, grad_all, weight_out, width, jnp.float32) + given[part].astype(jnp.float32)
        last = total.astype(jnp.bfloat16)
        sums.append(total)
        arrived.append([lax.ppermute(last, "col", hop) for hop in hops])
    before = input_pieces()
    input_steps(quarter, last)
    grad_weight_out = weight_out_grad_piece(after(act, last, *before), grad_all, 0, 2, None)

    hid_pieces, where, partial, far = [], [], grad_weight_out, None
    for part in range(parts):
        arrived[part], partial, *_ = lax.optimization_barrier((arrived[part], partial, *input_pieces()))
        if part == 0:
            grad_weight_out, partial = partial, None
        total = sums[part]
        for value in arrived[part]:
            total = total + value.astype(jnp.float32)
        mine = (total * slope[:, part * width : (part + 1) * width]).astype(jnp.bfloat16)
        other = [lax.ppermute(piece, "col", twin) for piece in jnp.split(mine, 2)]
        end = part == parts - 1
        input_steps(rows if end else quarter, mine)
        here = at(core * parts + part, (1 - core) * parts + part)
        made = input_grad_piece(here, mine, other, weight_in, partial, share, steps if end else None)
        partial = made[0]
        if end:
            far = made[1]
        hid_pieces += [[mine], other]
        where += [core * parts + part, (1 - core) * parts + part]
    input_all = input_pieces()
    where = at(*where)

    tile = tile_of(inputs.shape[1], 256)
    tiles = inputs.shape[1] // tile
    plan = [1, 1, 6, 12] if steps == 4 else [12] * steps
    state = {"in": None, "out": grad_weight_out, "first": 0, "calls": 0}

    def block(shift):
        spot = shift % rows * share
        return far if shift == steps else partial[spot : spot + share]

    def fill(sent, received):
        call = state["calls"]
        state["calls"] += 1
        if call == min(1, steps - 1):
            state["out"] = weight_out_grad_piece(after(act, *sent), grad_all, 1, 2, state["out"])
            received, state["out"] = lax.optimization_barrier((received, state["out"]))
        count = min(tiles * plan[call] // 12, tiles) - state["first"]
        if count > 0:
            state["in"] = weight_in_grad_piece(
                after(where, *sent), input_all, hid_pieces, state["first"], count, tile, state["in"]
            )
            state["first"] += count
            received, state["in"] = lax.optimization_barrier((received, state["in"]))
        return received

    grad_in = ring_sum(block, cycle, share, inputs.shape[1], jnp.bfloat16, fill)
    return (grad_in, state["in"], state["out"])


def solution(mesh):
    return jax.shard_map(
        functools.partial(body, row_cycle(mesh)),
        mesh=mesh,
        in_specs=(
            P("row", "col"),
            P(None, "row"),
            P("row", "col"),
            P("col", "row"),
            P("row", "col"),
        ),
        out_specs=(P("row", "col"), P("col", "row"), P("row", "col")),
        check_vma=False,
    )
```

```python
import functools

import jax
import jax.numpy as jnp
from jax import lax
from jax.experimental import pallas as pl
from jax.experimental.pallas import tpu as pltpu
from jax.sharding import PartitionSpec as P

VMEM_BYTES = 20 * 2**20
STREAM_VMEM_BYTES = 47 * 2**20


def row_cycle(mesh):
    first = mesh.devices[:, 0]
    places = [getattr(device, "coords", None) for device in first]
    if any(place is None for place in places):
        return list(range(len(first)))
    at = {(place[2], place[1]): index for index, place in enumerate(places)}
    zs, ys = (sorted({key[i] for key in at}) for i in (0, 1))
    if len(at) != len(places) or len(at) != len(zs) * len(ys) or len(ys) < 2:
        return list(range(len(first)))
    walk = []
    for step, z in enumerate(zs):
        walk += [at[z, y] for y in (ys[1:] if step % 2 == 0 else ys[:0:-1])]
    return walk + [at[z, ys[0]] for z in reversed(zs)]


def pieces_of(length, want):
    return max(n for n in range(1, want + 1) if length % (128 * n) == 0 or n == 1)


def tile_of(length, most):
    return max(t for t in range(1, most + 1) if length % t == 0 and (t % 128 == 0 or t == length))


def gelu_parts(hidden_pre):
    hval = hidden_pre.astype(jnp.float32)
    inner = 0.7978845608 * (hval + 0.044715 * hval * hval * hval)
    tval = jnp.tanh(inner)
    act = 0.5 * hval * (1.0 + tval)
    slope = 0.5 * (1.0 + tval) + 0.5 * hval * (1.0 - tval * tval) * 0.7978845608 * (
        1.0 + 3.0 * 0.044715 * hval * hval
    )
    return (act, slope)


def gelu_blocks(order, hidden_pre, count):
    tokens, hidden = hidden_pre.shape
    share = tokens // count
    half = hidden // 2

    def kernel(order_ref, h_ref, act_ref, slope_ref, mark_ref):
        mark_ref[...] = jnp.zeros_like(mark_ref)
        for index in range(2):
            at = slice(index * half, (index + 1) * half)

            @pl.when(order_ref[count] == index)
            def _():
                act, slope = gelu_parts(h_ref[:, at])
                act_ref[:, at] = act.astype(jnp.bfloat16)
                slope_ref[...] = slope

            @pl.when(order_ref[count] != index)
            def _():
                act_ref[:, at] = gelu_parts(h_ref[:, at])[0].astype(jnp.bfloat16)

    return pl.pallas_call(
        kernel,
        grid_spec=pltpu.PrefetchScalarGridSpec(
            num_scalar_prefetch=1,
            grid=(count,),
            in_specs=[pl.BlockSpec((share, hidden), lambda i, s: (s[i], 0))],
            out_specs=[
                pl.BlockSpec((share, hidden), lambda i, s: (i, 0)),
                pl.BlockSpec((share, half), lambda i, s: (i, 0)),
                pl.BlockSpec((8, 128), lambda i, s: (0, 0)),
            ],
        ),
        out_shape=[
            pltpu.HBM((tokens, hidden), jnp.bfloat16),
            pltpu.HBM((tokens, half), jnp.float32),
            jax.ShapeDtypeStruct((8, 128), jnp.float32),
        ],
        compiler_params=pltpu.CompilerParams(vmem_limit_bytes=VMEM_BYTES),
        cost_estimate=cost(20 * tokens * hidden, 6 * tokens * hidden),
        name="gelu_blocks",
    )(order, hidden_pre)


def after(value, *others):
    return lax.optimization_barrier((value, *others))[0]


def ring_gather(value, cycle):
    count = len(cycle)
    ahead = [(cycle[i], cycle[(i + 1) % count]) for i in range(count)]
    behind = [(b, a) for a, b in ahead]
    blocks = {0: [value]}
    state = [value, value]

    def step(k, *others):
        fore, back = state
        if 2 * k == count:
            cut = value.shape[0] // 2
            fore, back = fore[:cut], back[cut:]
        if others:
            fore, back = lax.optimization_barrier((fore, back, *others))[:2]
        state[:] = lax.ppermute(fore, "row", ahead), lax.ppermute(back, "row", behind)
        share = value.shape[0]
        if 2 * k == count:
            blocks[k] = list(state)
            return [(k * share, state[0]), (k * share + cut, state[1])]
        blocks[count - k], blocks[k] = [state[0]], [state[1]]
        return [((count - k) * share, state[0]), (k * share, state[1])]

    return step, lambda: [piece for k in sorted(blocks) for piece in blocks[k]]


def ring_sum(block, cycle, share, width, dtype, fill):
    count = len(cycle)
    half = width // 2
    ahead = [(cycle[i], cycle[(i + 1) % count]) for i in range(count)]
    behind = [(b, a) for a, b in ahead]

    def plus(left, right):
        return left.astype(jnp.float32) + right.astype(jnp.float32)

    def move(first, second):
        sent = (first.astype(jnp.bfloat16), second.astype(jnp.bfloat16))
        return fill(sent, (lax.ppermute(sent[0], "row", ahead), lax.ppermute(sent[1], "row", behind)))

    most = count // 2
    if count == 1:
        return block(0).astype(dtype)
    fore = back = None
    if count % 2 == 0:
        far = block(most)
        fore, back = move(far[:, :half], far[:, half:])
        most -= 1
    for shift in range(most, 0, -1):
        first, second = block(shift), block(-shift)
        if fore is not None and fore.shape[1] < width:
            fore = jnp.pad(fore, ((0, 0), (0, width - half)))
            back = jnp.pad(back, ((0, 0), (half, 0)))
        if fore is not None:
            first, second = plus(first, fore), plus(second, back)
        fore, back = move(first, second)
    own = block(0)
    if fore.shape[1] < width:
        return jnp.concatenate([plus(own[:, :half], fore), plus(own[:, half:], back)], 1).astype(dtype)
    return (plus(own, fore) + back.astype(jnp.float32)).astype(dtype)


def cost(flops, moved):
    return pl.CostEstimate(flops=flops // 4, bytes_accessed=moved // 4, transcendentals=0)


NEAR = pl.BlockSpec(memory_space=pltpu.VMEM)
FAR = pl.BlockSpec(memory_space=pltpu.HBM)
SCALAR = pl.BlockSpec(memory_space=pltpu.SMEM)
LAST_DIMS = (((1,), (1,)), ((), ()))


def run_of(length, first):
    return [(0, first), (first, length - first)] if first < length else [(0, length)]


def near_rows(start, weight, width):
    def kernel(start_ref, w_ref, o_ref, sem):
        rows = pl.ds(pl.multiple_of(start_ref[0] * width, width), width)
        copy = pltpu.make_async_copy(w_ref.at[rows], o_ref, sem)
        copy.start()
        copy.wait()

    return pl.pallas_call(
        kernel,
        in_specs=[SCALAR, FAR],
        out_specs=NEAR,
        out_shape=pltpu.VMEM((width, weight.shape[1]), weight.dtype),
        scratch_shapes=[pltpu.SemaphoreType.DMA],
        compiler_params=pltpu.CompilerParams(vmem_limit_bytes=STREAM_VMEM_BYTES),
        cost_estimate=cost(0, 4 * width * weight.shape[1]),
        name="near_rows",
    )(start, weight)


def near_grad_piece(grads, rows, taken):
    def kernel(g_ref, w_ref, *refs):
        value = lax.dot_general(g_ref[...], w_ref[...], LAST_DIMS, preferred_element_type=jnp.float32)
        if taken is not None:
            value += refs[0][...].astype(jnp.float32)
            refs[1][...] = value
        refs[-1][...] = value.astype(jnp.bfloat16)

    shape = (grads.shape[0], rows.shape[0])
    sent = jax.ShapeDtypeStruct(shape, jnp.bfloat16)
    return pl.pallas_call(
        kernel,
        in_specs=[NEAR, NEAR] + ([] if taken is None else [NEAR]),
        out_specs=NEAR if taken is None else [NEAR, NEAR],
        out_shape=sent if taken is None else [jax.ShapeDtypeStruct(shape, jnp.float32), sent],
        compiler_params=pltpu.CompilerParams(vmem_limit_bytes=12 * 2**20),
        cost_estimate=cost(2 * grads.shape[1] * shape[0] * shape[1], 2 * rows.shape[0] * rows.shape[1]),
        name="near_grad_piece",
    )(grads, rows, *([] if taken is None else [taken]))


def act_grad_piece(start, grads, weight_out, width, dtype):
    tokens, depth = grads.shape
    runs = run_of(width, tile_of(width, 256))

    def kernel(start_ref, g_ref, w_ref, o_ref, near, sem):
        copies = [
            pltpu.make_async_copy(
                w_ref.at[pl.ds(pl.multiple_of(start_ref[0] * width + at, 128), size)],
                near.at[pl.ds(at, size)],
                sem.at[index],
            )
            for index, (at, size) in enumerate(runs)
        ]
        for copy in copies:
            copy.start()
        for copy, (at, size) in zip(copies, runs):
            copy.wait()
            o_ref[:, at : at + size] = lax.dot_general(
                g_ref[...], near[at : at + size, :], LAST_DIMS, preferred_element_type=jnp.float32
            ).astype(dtype)

    return pl.pallas_call(
        kernel,
        in_specs=[SCALAR, NEAR, FAR],
        out_specs=NEAR,
        out_shape=jax.ShapeDtypeStruct((tokens, width), dtype),
        scratch_shapes=[pltpu.VMEM((width, depth), jnp.bfloat16), pltpu.SemaphoreType.DMA((len(runs),))],
        compiler_params=pltpu.CompilerParams(vmem_limit_bytes=STREAM_VMEM_BYTES),
        cost_estimate=cost(2 * tokens * depth * width, 2 * width * depth + 4 * tokens * width),
        name="act_grad_piece",
    )(start, grads, weight_out)


def input_grad_piece(where, mine, other, weight_in, total, share, far):
    tokens, width = mine.shape
    out = weight_in.shape[0]
    tile = tile_of(out, 768)

    def kernel(_, m_ref, *refs):
        theirs = jnp.concatenate([ref[...] for ref in refs[: len(other)]], 0)
        wm_ref, wo_ref, *refs = refs[len(other) :]
        value = lax.dot_general(m_ref[...], wm_ref[...], LAST_DIMS, preferred_element_type=jnp.float32)
        value += lax.dot_general(theirs, wo_ref[...], LAST_DIMS, preferred_element_type=jnp.float32)
        if total is not None:
            value += refs[0][...]
            refs = refs[1:]
        refs[0][...] = value
        if far is not None:
            refs[1][...] = value[far * share : (far + 1) * share].astype(jnp.bfloat16)

    block = pl.BlockSpec((tokens, tile), lambda i, s: (0, i))
    out_specs, out_shape = [block], [jax.ShapeDtypeStruct((tokens, out), jnp.float32)]
    if far is not None:
        out_specs.append(pl.BlockSpec((share, tile), lambda i, s: (0, i)))
        out_shape.append(jax.ShapeDtypeStruct((share, out), jnp.bfloat16))
    return pl.pallas_call(
        kernel,
        grid_spec=pltpu.PrefetchScalarGridSpec(
            num_scalar_prefetch=1,
            grid=(out // tile,),
            in_specs=[NEAR] * (1 + len(other))
            + [
                pl.BlockSpec((tile, width), lambda i, s: (i, s[0])),
                pl.BlockSpec((tile, width), lambda i, s: (i, s[1])),
            ]
            + ([] if total is None else [block]),
            out_specs=out_specs,
        ),
        out_shape=out_shape,
        compiler_params=pltpu.CompilerParams(vmem_limit_bytes=STREAM_VMEM_BYTES),
        cost_estimate=cost(4 * tokens * width * out, 4 * width * out + 8 * tokens * out),
        name="input_grad_piece",
    )(where, mine, *other, weight_in, weight_in, *([] if total is None else [total]))


def weight_out_grad_piece(act, grads, part, parts, held):
    tokens, rows = act.shape
    columns = grads.shape[1]
    share = rows // parts
    tile = tile_of(share, 512)
    first = part * (share // tile)

    def kernel(a_ref, g_ref, *refs):
        refs[-1][...] = lax.dot_general(
            a_ref[...], g_ref[...], (((0,), (0,)), ((), ())), preferred_element_type=jnp.float32
        ).astype(jnp.bfloat16)

    return pl.pallas_call(
        kernel,
        grid=(share // tile,),
        in_specs=[
            pl.BlockSpec((tokens, tile), lambda i: (0, first + i)),
            NEAR,
        ]
        + ([] if held is None else [pl.BlockSpec(memory_space=pl.ANY)]),
        out_specs=pl.BlockSpec((tile, columns), lambda i: (first + i, 0)),
        out_shape=jax.ShapeDtypeStruct((rows, columns), jnp.bfloat16),
        input_output_aliases={} if held is None else {2: 0},
        compiler_params=pltpu.CompilerParams(vmem_limit_bytes=VMEM_BYTES),
        cost_estimate=cost(2 * tokens * share * columns, 2 * share * columns + 2 * tokens * columns),
        name="weight_out_grad_piece",
    )(act, grads, *([] if held is None else [held]))


def near_hidden(where, hid_pieces):
    width = hid_pieces[0][0].shape[1]
    blocks = [block for piece in hid_pieces for block in piece]
    places = []
    for index, piece in enumerate(hid_pieces):
        row = 0
        for block in piece:
            places.append((index, row, block.shape[0]))
            row += block.shape[0]

    def kernel(where_ref, *refs):
        out_ref, sem = refs[-2:]
        copies = []
        for spot, (index, row, size) in enumerate(places):
            columns = pl.ds(pl.multiple_of(where_ref[index] * width, 128), width)
            copies.append(
                pltpu.make_async_copy(refs[spot], out_ref.at[pl.ds(row, size), columns], sem.at[spot])
            )
        for copy in copies:
            copy.start()
        for copy in copies:
            copy.wait()

    shape = (sum(block.shape[0] for block in hid_pieces[0]), width * len(hid_pieces))
    return pl.pallas_call(
        kernel,
        in_specs=[SCALAR] + [pl.BlockSpec(memory_space=pl.ANY)] * len(blocks),
        out_specs=NEAR,
        out_shape=pltpu.VMEM(shape, blocks[0].dtype),
        scratch_shapes=[pltpu.SemaphoreType.DMA((len(blocks),))],
        compiler_params=pltpu.CompilerParams(vmem_limit_bytes=2**20),
        cost_estimate=cost(0, 4 * shape[0] * shape[1]),
        name="near_hidden",
    )(where, *blocks)


def weight_in_grad_piece(hidden, input_pieces, first, tiles, tile, held):
    rows = input_pieces[0].shape[1]
    tokens, columns = hidden.shape
    blocks = len(input_pieces)

    def kernel(h_ref, *refs):
        left = jnp.concatenate([ref[...] for ref in refs[:blocks]], 0).T
        refs[-1][...] = jnp.dot(left, h_ref[...], preferred_element_type=jnp.float32).astype(jnp.bfloat16)

    return pl.pallas_call(
        kernel,
        grid=(tiles,),
        in_specs=[NEAR]
        + [pl.BlockSpec((piece.shape[0], tile), lambda i: (0, first + i)) for piece in input_pieces]
        + ([] if held is None else [pl.BlockSpec(memory_space=pl.ANY)]),
        out_specs=pl.BlockSpec((tile, columns), lambda i: (first + i, 0)),
        out_shape=jax.ShapeDtypeStruct((rows, columns), jnp.bfloat16),
        input_output_aliases={} if held is None else {1 + blocks: 0},
        compiler_params=pltpu.CompilerParams(vmem_limit_bytes=VMEM_BYTES),
        cost_estimate=cost(2 * tokens * tiles * tile * columns, 2 * tiles * tile * columns),
        name="weight_in_grad_piece",
    )(hidden, *input_pieces, *([] if held is None else [held]))


def body(cycle, inputs, hidden_pre, out_grad, weight_in, weight_out):
    cols = lax.axis_size("col")
    core = lax.axis_index("col") % 2
    twin = [(i, i ^ 1) for i in range(cols)]
    hops = [[(i, (i + 2 * hop) % cols) for i in range(cols)] for hop in range(1, cols // 2)]
    rows, share = len(cycle), out_grad.shape[0]
    place = lax.axis_index("row")
    order = [
        sum(jnp.where(place == row, cycle[(spot + shift) % rows], 0) for spot, row in enumerate(cycle))
        for shift in range(rows)
    ]
    half = hidden_pre.shape[1] // 2
    parts = pieces_of(half, 2)
    width = half // parts

    def at(*indices):
        return jnp.stack(indices).astype(jnp.int32)

    steps = rows // 2
    order = at(*order, core)
    grad_step, grad_pieces = ring_gather(out_grad, cycle)
    grad_all = jnp.zeros((rows * share, out_grad.shape[1]), out_grad.dtype)

    def put(pieces):
        whole = grad_all
        for start, piece in pieces:
            whole = lax.dynamic_update_slice_in_dim(whole, piece, start, 0)
        return whole

    new, loaded = [(0, out_grad)], []
    act = slope = mark = None
    for k in range(1, steps + 1):
        fresh = grad_step(k, *([] if k == 1 else [mark, grad_all, *loaded]))
        if k == 1:
            act, slope, mark = gelu_blocks(order, hidden_pre, rows)
        grad_all = put(new)
        for index in {2: range(parts), 3: range(parts, parts + 1)}.get(k, ()):
            side = 1 - core if index < parts else core
            start = after(at(side * parts + index % parts), grad_all, *loaded)
            loaded.append(near_rows(start, weight_out, width))
        new = fresh
    grad_all = put(new)
    grad_all = after(grad_all, mark)
    input_step, input_pieces = ring_gather(inputs, cycle)
    due = list(range(1, steps + 1))

    quarter = max(1, steps // 4)

    def input_steps(count, *others):
        for _ in range(min(count, len(due))):
            input_step(due.pop(0), *others)

    given, last = [], grad_all
    for part in range(parts):
        last = near_grad_piece(grad_all, after(loaded[part], last), None)
        given.append(lax.ppermute(last, "col", twin))
    input_steps(quarter, last)
    sums, arrived = [], []
    for part in range(parts):
        if parts + part < len(loaded):
            total, last = near_grad_piece(grad_all, after(loaded[parts + part], last), given[part])
        else:
            start = after(at(core * parts + part), last)
            kept = act_grad_piece(start, grad_all, weight_out, width, jnp.float32)
            total = kept + given[part].astype(jnp.float32)
            last = total.astype(jnp.bfloat16)
        sums.append(total)
        arrived.append([lax.ppermute(last, "col", hop) for hop in hops])
    before = input_pieces()
    input_steps(quarter, last)
    grad_weight_out = weight_out_grad_piece(after(act, last, *before), grad_all, 0, 2, None)

    hid_pieces, where, partial, far = [], [], grad_weight_out, None
    for part in range(parts):
        arrived[part], partial, *_ = lax.optimization_barrier((arrived[part], partial, *input_pieces()))
        if part == 0:
            grad_weight_out, partial = partial, None
        total = sums[part]
        for value in arrived[part]:
            total = total + value.astype(jnp.float32)
        mine = (total * slope[:, part * width : (part + 1) * width]).astype(jnp.bfloat16)
        other = [lax.ppermute(piece, "col", twin) for piece in jnp.split(mine, 2)]
        end = part == parts - 1
        input_steps(rows if end else quarter, mine)
        here = at(core * parts + part, (1 - core) * parts + part)
        made = input_grad_piece(here, mine, other, weight_in, partial, share, steps if end else None)
        partial = made[0]
        if end:
            far = made[1]
        hid_pieces += [[mine], other]
        where += [core * parts + part, (1 - core) * parts + part]
    input_all = input_pieces()
    where = at(*where)

    tile = tile_of(inputs.shape[1], 256)
    tiles = inputs.shape[1] // tile
    plan = [2, 2, 7, 12] if steps == 4 else [12] * steps
    state = {"hidden": None, "in": None, "out": grad_weight_out, "first": 0, "calls": 0}

    def block(shift):
        spot = shift % rows * share
        return far if shift == steps else partial[spot : spot + share]

    def fill(sent, received):
        call = state["calls"]
        state["calls"] += 1
        if call == min(1, steps - 1):
            state["out"] = weight_out_grad_piece(after(act, *sent), grad_all, 1, 2, state["out"])
            received, state["out"] = lax.optimization_barrier((received, state["out"]))
        count = min(tiles * plan[call] // 12, tiles) - state["first"]
        if count > 0:
            if state["hidden"] is None:
                state["hidden"] = near_hidden(after(where, *sent), hid_pieces)
            state["in"] = weight_in_grad_piece(
                after(state["hidden"], *sent), input_all, state["first"], count, tile, state["in"]
            )
            state["first"] += count
            received, state["in"] = lax.optimization_barrier((received, state["in"]))
        return received

    grad_in = ring_sum(block, cycle, share, inputs.shape[1], jnp.bfloat16, fill)
    return (grad_in, state["in"], state["out"])


def solution(mesh):
    return jax.shard_map(
        functools.partial(body, row_cycle(mesh)),
        mesh=mesh,
        in_specs=(
            P("row", "col"),
            P(None, "row"),
            P("row", "col"),
            P("col", "row"),
            P("row", "col"),
        ),
        out_specs=(P("row", "col"), P("col", "row"), P("row", "col")),
        check_vma=False,
    )
```

```python
import functools

import jax
import jax.numpy as jnp
from jax import lax
from jax.experimental import pallas as pl
from jax.experimental.pallas import tpu as pltpu
from jax.sharding import PartitionSpec as P

VMEM_BYTES = 20 * 2**20
STREAM_VMEM_BYTES = 47 * 2**20
SUM_VMEM_BYTES = 41 * 2**20


def row_cycle(mesh):
    first = mesh.devices[:, 0]
    places = [getattr(device, "coords", None) for device in first]
    if any(place is None for place in places):
        return list(range(len(first)))
    at = {(place[2], place[1]): index for index, place in enumerate(places)}
    zs, ys = (sorted({key[i] for key in at}) for i in (0, 1))
    if len(at) != len(places) or len(at) != len(zs) * len(ys) or len(ys) < 2:
        return list(range(len(first)))
    walk = []
    for step, z in enumerate(zs):
        walk += [at[z, y] for y in (ys[1:] if step % 2 == 0 else ys[:0:-1])]
    return walk + [at[z, ys[0]] for z in reversed(zs)]


def pieces_of(length, want):
    return max(n for n in range(1, want + 1) if length % (128 * n) == 0 or n == 1)


def tile_of(length, most):
    return max(t for t in range(1, most + 1) if length % t == 0 and (t % 128 == 0 or t == length))


def gelu_parts(hidden_pre):
    hval = hidden_pre.astype(jnp.float32)
    inner = 0.7978845608 * (hval + 0.044715 * hval * hval * hval)
    tval = jnp.tanh(inner)
    act = 0.5 * hval * (1.0 + tval)
    slope = 0.5 * (1.0 + tval) + 0.5 * hval * (1.0 - tval * tval) * 0.7978845608 * (
        1.0 + 3.0 * 0.044715 * hval * hval
    )
    return (act, slope)


def gelu_blocks(order, hidden_pre, count):
    tokens, hidden = hidden_pre.shape
    share = tokens // count
    half = hidden // 2

    def kernel(order_ref, h_ref, act_ref, slope_ref, mark_ref):
        mark_ref[...] = jnp.zeros_like(mark_ref)
        for index in range(2):
            at = slice(index * half, (index + 1) * half)

            @pl.when(order_ref[count] == index)
            def _():
                act, slope = gelu_parts(h_ref[:, at])
                act_ref[:, at] = act.astype(jnp.bfloat16)
                slope_ref[...] = slope

            @pl.when(order_ref[count] != index)
            def _():
                act_ref[:, at] = gelu_parts(h_ref[:, at])[0].astype(jnp.bfloat16)

    return pl.pallas_call(
        kernel,
        grid_spec=pltpu.PrefetchScalarGridSpec(
            num_scalar_prefetch=1,
            grid=(count,),
            in_specs=[pl.BlockSpec((share, hidden), lambda i, s: (s[i], 0))],
            out_specs=[
                pl.BlockSpec((share, hidden), lambda i, s: (i, 0)),
                pl.BlockSpec((share, half), lambda i, s: (i, 0)),
                pl.BlockSpec((8, 128), lambda i, s: (0, 0)),
            ],
        ),
        out_shape=[
            pltpu.HBM((tokens, hidden), jnp.bfloat16),
            pltpu.HBM((tokens, half), jnp.float32),
            jax.ShapeDtypeStruct((8, 128), jnp.float32),
        ],
        compiler_params=pltpu.CompilerParams(vmem_limit_bytes=VMEM_BYTES),
        cost_estimate=cost(20 * tokens * hidden, 6 * tokens * hidden),
        name="gelu_blocks",
    )(order, hidden_pre)


def after(value, *others):
    return lax.optimization_barrier((value, *others))[0]


def ring_gather(value, cycle):
    count = len(cycle)
    ahead = [(cycle[i], cycle[(i + 1) % count]) for i in range(count)]
    behind = [(b, a) for a, b in ahead]
    blocks = {0: [value]}
    state = [value, value]

    def step(k, *others):
        fore, back = state
        if 2 * k == count:
            cut = value.shape[0] // 2
            fore, back = fore[:cut], back[cut:]
        if others:
            fore, back = lax.optimization_barrier((fore, back, *others))[:2]
        state[:] = lax.ppermute(fore, "row", ahead), lax.ppermute(back, "row", behind)
        share = value.shape[0]
        if 2 * k == count:
            blocks[k] = list(state)
            return [(k * share, state[0]), (k * share + cut, state[1])]
        blocks[count - k], blocks[k] = [state[0]], [state[1]]
        return [((count - k) * share, state[0]), (k * share, state[1])]

    return step, lambda: [piece for k in sorted(blocks) for piece in blocks[k]]


def ring_sum(block, cycle, share, width, dtype, fill):
    count = len(cycle)
    half = width // 2
    ahead = [(cycle[i], cycle[(i + 1) % count]) for i in range(count)]
    behind = [(b, a) for a, b in ahead]

    def plus(left, right):
        return left.astype(jnp.float32) + right.astype(jnp.float32)

    def move(first, second):
        sent = (first.astype(jnp.bfloat16), second.astype(jnp.bfloat16))
        return fill(sent, (lax.ppermute(sent[0], "row", ahead), lax.ppermute(sent[1], "row", behind)))

    most = count // 2
    if count == 1:
        return block(0).astype(dtype)
    fore = back = None
    if count % 2 == 0:
        far = block(most)
        fore, back = move(far[:, :half], far[:, half:])
        most -= 1
    for shift in range(most, 0, -1):
        first, second = block(shift), block(-shift)
        if fore is not None and fore.shape[1] < width:
            fore = jnp.pad(fore, ((0, 0), (0, width - half)))
            back = jnp.pad(back, ((0, 0), (half, 0)))
        if fore is not None:
            first, second = plus(first, fore), plus(second, back)
        fore, back = move(first, second)
    own = block(0)
    if fore.shape[1] < width:
        return jnp.concatenate([plus(own[:, :half], fore), plus(own[:, half:], back)], 1).astype(dtype)
    return (plus(own, fore) + back.astype(jnp.float32)).astype(dtype)


def cost(flops, moved):
    return pl.CostEstimate(flops=flops // 4, bytes_accessed=moved // 4, transcendentals=0)


NEAR = pl.BlockSpec(memory_space=pltpu.VMEM)
FAR = pl.BlockSpec(memory_space=pltpu.HBM)
SCALAR = pl.BlockSpec(memory_space=pltpu.SMEM)
LAST_DIMS = (((1,), (1,)), ((), ()))


def run_of(length, first):
    return [(0, first), (first, length - first)] if first < length else [(0, length)]


def near_rows(start, weight, width):
    def kernel(start_ref, w_ref, o_ref, sem):
        rows = pl.ds(pl.multiple_of(start_ref[0] * width, width), width)
        copy = pltpu.make_async_copy(w_ref.at[rows], o_ref, sem)
        copy.start()
        copy.wait()

    return pl.pallas_call(
        kernel,
        in_specs=[SCALAR, FAR],
        out_specs=NEAR,
        out_shape=pltpu.VMEM((width, weight.shape[1]), weight.dtype),
        scratch_shapes=[pltpu.SemaphoreType.DMA],
        compiler_params=pltpu.CompilerParams(vmem_limit_bytes=STREAM_VMEM_BYTES),
        cost_estimate=cost(0, 4 * width * weight.shape[1]),
        name="near_rows",
    )(start, weight)


def near_grad_piece(grads, rows, taken):
    def kernel(g_ref, w_ref, *refs):
        value = lax.dot_general(g_ref[...], w_ref[...], LAST_DIMS, preferred_element_type=jnp.float32)
        if taken is not None:
            value += refs[0][...].astype(jnp.float32)
            refs[1][...] = value
        refs[-1][...] = value.astype(jnp.bfloat16)

    shape = (grads.shape[0], rows.shape[0])
    sent = jax.ShapeDtypeStruct(shape, jnp.bfloat16)
    return pl.pallas_call(
        kernel,
        in_specs=[NEAR, NEAR] + ([] if taken is None else [NEAR]),
        out_specs=NEAR if taken is None else [NEAR, NEAR],
        out_shape=sent if taken is None else [jax.ShapeDtypeStruct(shape, jnp.float32), sent],
        compiler_params=pltpu.CompilerParams(vmem_limit_bytes=12 * 2**20),
        cost_estimate=cost(2 * grads.shape[1] * shape[0] * shape[1], 2 * rows.shape[0] * rows.shape[1]),
        name="near_grad_piece",
    )(grads, rows, *([] if taken is None else [taken]))


def act_grad_piece(start, grads, weight_out, width, dtype):
    tokens, depth = grads.shape
    runs = run_of(width, tile_of(width, 256))

    def kernel(start_ref, g_ref, w_ref, o_ref, near, sem):
        copies = [
            pltpu.make_async_copy(
                w_ref.at[pl.ds(pl.multiple_of(start_ref[0] * width + at, 128), size)],
                near.at[pl.ds(at, size)],
                sem.at[index],
            )
            for index, (at, size) in enumerate(runs)
        ]
        for copy in copies:
            copy.start()
        for copy, (at, size) in zip(copies, runs):
            copy.wait()
            o_ref[:, at : at + size] = lax.dot_general(
                g_ref[...], near[at : at + size, :], LAST_DIMS, preferred_element_type=jnp.float32
            ).astype(dtype)

    return pl.pallas_call(
        kernel,
        in_specs=[SCALAR, NEAR, FAR],
        out_specs=NEAR,
        out_shape=jax.ShapeDtypeStruct((tokens, width), dtype),
        scratch_shapes=[pltpu.VMEM((width, depth), jnp.bfloat16), pltpu.SemaphoreType.DMA((len(runs),))],
        compiler_params=pltpu.CompilerParams(vmem_limit_bytes=STREAM_VMEM_BYTES),
        cost_estimate=cost(2 * tokens * depth * width, 2 * width * depth + 4 * tokens * width),
        name="act_grad_piece",
    )(start, grads, weight_out)


def input_grad_piece(where, mine, other, weight_in, total, share, far):
    tokens, width = mine.shape
    out = weight_in.shape[0]
    tile = tile_of(out, 768)

    def kernel(_, m_ref, *refs):
        theirs = jnp.concatenate([ref[...] for ref in refs[: len(other)]], 0)
        wm_ref, wo_ref, *refs = refs[len(other) :]
        value = lax.dot_general(m_ref[...], wm_ref[...], LAST_DIMS, preferred_element_type=jnp.float32)
        value += lax.dot_general(theirs, wo_ref[...], LAST_DIMS, preferred_element_type=jnp.float32)
        here = pl.ds(pl.multiple_of(pl.program_id(0) * tile, tile), tile)
        if total is not None:
            value += refs[0][:, here]
            refs = refs[1:]
        refs[0][:, here] = value
        if far is not None:
            refs[1][...] = value[far * share : (far + 1) * share].astype(jnp.bfloat16)

    out_specs, out_shape = [NEAR], [pltpu.VMEM((tokens, out), jnp.float32)]
    if far is not None:
        out_specs.append(pl.BlockSpec((share, tile), lambda i, s: (0, i)))
        out_shape.append(jax.ShapeDtypeStruct((share, out), jnp.bfloat16))
    return pl.pallas_call(
        kernel,
        grid_spec=pltpu.PrefetchScalarGridSpec(
            num_scalar_prefetch=1,
            grid=(out // tile,),
            in_specs=[NEAR] * (1 + len(other))
            + [
                pl.BlockSpec((tile, width), lambda i, s: (i, s[0])),
                pl.BlockSpec((tile, width), lambda i, s: (i, s[1])),
            ]
            + ([] if total is None else [NEAR]),
            out_specs=out_specs,
        ),
        out_shape=out_shape,
        input_output_aliases={} if total is None else {4 + len(other): 0},
        compiler_params=pltpu.CompilerParams(vmem_limit_bytes=SUM_VMEM_BYTES),
        cost_estimate=cost(4 * tokens * width * out, 4 * width * out + 8 * tokens * out),
        name="input_grad_piece",
    )(where, mine, *other, weight_in, weight_in, *([] if total is None else [total]))


def weight_out_grad_piece(act, grads, part, parts, held):
    tokens, rows = act.shape
    columns = grads.shape[1]
    share = rows // parts
    tile = tile_of(share, 512)
    first = part * (share // tile)

    def kernel(a_ref, g_ref, *refs):
        refs[-1][...] = lax.dot_general(
            a_ref[...], g_ref[...], (((0,), (0,)), ((), ())), preferred_element_type=jnp.float32
        ).astype(jnp.bfloat16)

    return pl.pallas_call(
        kernel,
        grid=(share // tile,),
        in_specs=[
            pl.BlockSpec((tokens, tile), lambda i: (0, first + i)),
            NEAR,
        ]
        + ([] if held is None else [pl.BlockSpec(memory_space=pl.ANY)]),
        out_specs=pl.BlockSpec((tile, columns), lambda i: (first + i, 0)),
        out_shape=jax.ShapeDtypeStruct((rows, columns), jnp.bfloat16),
        input_output_aliases={} if held is None else {2: 0},
        compiler_params=pltpu.CompilerParams(vmem_limit_bytes=VMEM_BYTES),
        cost_estimate=cost(2 * tokens * share * columns, 2 * share * columns + 2 * tokens * columns),
        name="weight_out_grad_piece",
    )(act, grads, *([] if held is None else [held]))


def near_hidden(where, hid_pieces):
    width = hid_pieces[0][0].shape[1]
    blocks = [block for piece in hid_pieces for block in piece]
    places = []
    for index, piece in enumerate(hid_pieces):
        row = 0
        for block in piece:
            places.append((index, row, block.shape[0]))
            row += block.shape[0]

    def kernel(where_ref, *refs):
        out_ref, sem = refs[-2:]
        copies = []
        for spot, (index, row, size) in enumerate(places):
            columns = pl.ds(pl.multiple_of(where_ref[index] * width, 128), width)
            copies.append(
                pltpu.make_async_copy(refs[spot], out_ref.at[pl.ds(row, size), columns], sem.at[spot])
            )
        for copy in copies:
            copy.start()
        for copy in copies:
            copy.wait()

    shape = (sum(block.shape[0] for block in hid_pieces[0]), width * len(hid_pieces))
    return pl.pallas_call(
        kernel,
        in_specs=[SCALAR] + [pl.BlockSpec(memory_space=pl.ANY)] * len(blocks),
        out_specs=NEAR,
        out_shape=pltpu.VMEM(shape, blocks[0].dtype),
        scratch_shapes=[pltpu.SemaphoreType.DMA((len(blocks),))],
        compiler_params=pltpu.CompilerParams(vmem_limit_bytes=2**20),
        cost_estimate=cost(0, 4 * shape[0] * shape[1]),
        name="near_hidden",
    )(where, *blocks)


def weight_in_grad_piece(hidden, input_pieces, first, tiles, tile, held):
    rows = input_pieces[0].shape[1]
    tokens, columns = hidden.shape
    blocks = len(input_pieces)

    def kernel(h_ref, *refs):
        left = jnp.concatenate([ref[...] for ref in refs[:blocks]], 0).T
        refs[-1][...] = jnp.dot(left, h_ref[...], preferred_element_type=jnp.float32).astype(jnp.bfloat16)

    return pl.pallas_call(
        kernel,
        grid=(tiles,),
        in_specs=[NEAR]
        + [pl.BlockSpec((piece.shape[0], tile), lambda i: (0, first + i)) for piece in input_pieces]
        + ([] if held is None else [pl.BlockSpec(memory_space=pl.ANY)]),
        out_specs=pl.BlockSpec((tile, columns), lambda i: (first + i, 0)),
        out_shape=jax.ShapeDtypeStruct((rows, columns), jnp.bfloat16),
        input_output_aliases={} if held is None else {1 + blocks: 0},
        compiler_params=pltpu.CompilerParams(vmem_limit_bytes=VMEM_BYTES),
        cost_estimate=cost(2 * tokens * tiles * tile * columns, 2 * tiles * tile * columns),
        name="weight_in_grad_piece",
    )(hidden, *input_pieces, *([] if held is None else [held]))


def body(cycle, inputs, hidden_pre, out_grad, weight_in, weight_out):
    cols = lax.axis_size("col")
    core = lax.axis_index("col") % 2
    twin = [(i, i ^ 1) for i in range(cols)]
    hops = [[(i, (i + 2 * hop) % cols) for i in range(cols)] for hop in range(1, cols // 2)]
    rows, share = len(cycle), out_grad.shape[0]
    place = lax.axis_index("row")
    order = [
        sum(jnp.where(place == row, cycle[(spot + shift) % rows], 0) for spot, row in enumerate(cycle))
        for shift in range(rows)
    ]
    half = hidden_pre.shape[1] // 2
    parts = pieces_of(half, 2)
    width = half // parts

    def at(*indices):
        return jnp.stack(indices).astype(jnp.int32)

    steps = rows // 2
    order = at(*order, core)
    grad_step, grad_pieces = ring_gather(out_grad, cycle)
    grad_all = jnp.zeros((rows * share, out_grad.shape[1]), out_grad.dtype)

    def put(pieces):
        whole = grad_all
        for start, piece in pieces:
            whole = lax.dynamic_update_slice_in_dim(whole, piece, start, 0)
        return whole

    new, loaded = [(0, out_grad)], []
    act = slope = mark = None
    for k in range(1, steps + 1):
        fresh = grad_step(k, *([] if k == 1 else [mark, grad_all, *loaded]))
        if k == 1:
            act, slope, mark = gelu_blocks(order, hidden_pre, rows)
        grad_all = put(new)
        for index in {2: range(parts), 3: range(parts, parts + 1)}.get(k, ()):
            side = 1 - core if index < parts else core
            start = after(at(side * parts + index % parts), grad_all, *loaded)
            loaded.append(near_rows(start, weight_out, width))
        new = fresh
    grad_all = put(new)
    grad_all = after(grad_all, mark)
    input_step, input_pieces = ring_gather(inputs, cycle)
    due = list(range(1, steps + 1))

    quarter = max(1, steps // 4)

    def input_steps(count, *others):
        for _ in range(min(count, len(due))):
            input_step(due.pop(0), *others)

    given, last = [], grad_all
    for part in range(parts):
        last = near_grad_piece(grad_all, after(loaded[part], last), None)
        given.append(lax.ppermute(last, "col", twin))
    input_steps(quarter, last)
    sums, arrived = [], []
    for part in range(parts):
        if parts + part < len(loaded):
            total, last = near_grad_piece(grad_all, after(loaded[parts + part], last), given[part])
        else:
            start = after(at(core * parts + part), last)
            kept = act_grad_piece(start, grad_all, weight_out, width, jnp.float32)
            total = kept + given[part].astype(jnp.float32)
            last = total.astype(jnp.bfloat16)
        sums.append(total)
        arrived.append([lax.ppermute(last, "col", hop) for hop in hops])
    before = input_pieces()
    input_steps(quarter, last)
    grad_weight_out = weight_out_grad_piece(after(act, last, *before), grad_all, 0, 2, None)

    hid_pieces, where, partial, far = [], [], grad_weight_out, None
    for part in range(parts):
        arrived[part], partial, *_ = lax.optimization_barrier((arrived[part], partial, *input_pieces()))
        if part == 0:
            grad_weight_out, partial = partial, None
        total = sums[part]
        for value in arrived[part]:
            total = total + value.astype(jnp.float32)
        mine = (total * slope[:, part * width : (part + 1) * width]).astype(jnp.bfloat16)
        other = [lax.ppermute(piece, "col", twin) for piece in jnp.split(mine, 2)]
        end = part == parts - 1
        input_steps(rows if end else quarter, mine)
        here = at(core * parts + part, (1 - core) * parts + part)
        made = input_grad_piece(here, mine, other, weight_in, partial, share, steps if end else None)
        partial = made[0]
        if end:
            far = made[1]
        hid_pieces += [[mine], other]
        where += [core * parts + part, (1 - core) * parts + part]
    input_all = input_pieces()
    where = at(*where)

    tile = tile_of(inputs.shape[1], 256)
    tiles = inputs.shape[1] // tile
    plan = [2, 2, 7, 12] if steps == 4 else [12] * steps
    state = {"hidden": None, "in": None, "out": grad_weight_out, "first": 0, "calls": 0}

    def block(shift):
        spot = shift % rows * share
        return far if shift == steps else partial[spot : spot + share]

    def fill(sent, received):
        call = state["calls"]
        state["calls"] += 1
        if call == min(1, steps - 1):
            state["out"] = weight_out_grad_piece(after(act, *sent), grad_all, 1, 2, state["out"])
            received, state["out"] = lax.optimization_barrier((received, state["out"]))
        count = min(tiles * plan[call] // 12, tiles) - state["first"]
        if count > 0:
            if state["hidden"] is None:
                state["hidden"] = near_hidden(after(where, *sent), hid_pieces)
            state["in"] = weight_in_grad_piece(
                after(state["hidden"], *sent), input_all, state["first"], count, tile, state["in"]
            )
            state["first"] += count
            received, state["in"] = lax.optimization_barrier((received, state["in"]))
        return received

    grad_in = ring_sum(block, cycle, share, inputs.shape[1], jnp.bfloat16, fill)
    return (grad_in, state["in"], state["out"])


def solution(mesh):
    return jax.shard_map(
        functools.partial(body, row_cycle(mesh)),
        mesh=mesh,
        in_specs=(
            P("row", "col"),
            P(None, "row"),
            P("row", "col"),
            P("col", "row"),
            P("row", "col"),
        ),
        out_specs=(P("row", "col"), P("col", "row"), P("row", "col")),
        check_vma=False,
    )
```
